32 devices in a mesh: scene: 4 (over y, x), tile: 8 (over z, core).
Axes of the slice: x: 2, y: 2, z: 4, core: 2. Of those that a mesh axis runs over, the one named last changes fastest.
Arguments:
- level0: bfloat16 [4, 8, 32, 32, 256], P('scene', 'tile'), may hold values from -6 to 6
- level1: bfloat16 [4, 8, 16, 16, 256], P('scene', 'tile'), may hold values from -6 to 6
- conv_weight: bfloat16 [3, 3, 256, 256], replicated, may hold values from -0.125 to 0.125
- deconv_weight: bfloat16 [2, 2, 256, 256], replicated, may hold values from -0.375 to 0.375
- mask_weight: bfloat16 [80, 256], replicated, may hold values from -0.375 to 0.375
- crop_level: int32 [4, 8, 24], P('scene', 'tile'), may hold values from 0 to 1
- crop_row: int32 [4, 8, 24], P('scene', 'tile'), may hold values from 0 to 18, as said below
- crop_col: int32 [4, 8, 24], P('scene', 'tile'), may hold values from 0 to 18, as said below
- roi_slot: int32 [4, 8, 22], P('scene', 'tile'), may hold values from 0 to 23, as said below
- roi_class: int32 [4, 8, 22], P('scene', 'tile'), may hold values from 0 to 79
- mask_target: int32 [4, 8, 22, 28, 28], P('scene', 'tile'), may hold values 0 or 1
Outputs:
- grad_level0: float32 [4, 8, 32, 32, 256], P('scene', 'tile')
- grad_level1: float32 [4, 8, 16, 16, 256], P('scene', 'tile')
- grad_mask: float32 [80, 256], P(None, 'tile')
- roi_loss: float32 [4, 8, 22], P('scene', 'tile')
The draws below stay inside these ranges and needn't reach their ends.
Inputs may be any that keep to these rules, and one draw needn't show every extreme that they name: `roi_slot`: each entry is tile * 3 + k with k < 3; the 22 entries of one head owner are distinct; a head owner takes at most 3 RoIs from one tile, and some head owner takes exactly 3 from some tile. A crop lies inside the tile of its level: crop_row + 14 is at most 32 for level 0 and 16 for level 1. A crop lies inside the tile of its level: crop_col + 14 is at most 32 for level 0 and 16 for level 1.
All inputs are finite; a program needn't handle non-finite values. No bound on the sum of `mask_target` on one device may be relied on, other than what follows from the above.
Results may differ from the reference program's by a relative error of at most 0.0053.
Values may be sent and summed in bfloat16 or wider, within the bound.
A program may use at most 192 MiB of HBM per device.

```python
import jax
import jax.numpy as jnp
from jax import lax

CH = 256
CLASSES = 80
CROP = 14
OUT = 28
T0 = 32
T1 = 16
R_DEV = 22
CAP = 3
N_SCENE = 4
N_TILE = 8


def crop_frame(key):
    key_level, key_row, key_col = jax.random.split(key, 3)
    grid_shape = (N_SCENE, N_TILE, N_TILE * CAP)
    levels = jax.random.randint(key_level, grid_shape, 0, 2, dtype=jnp.int32)
    levels = levels.at[:, :, 0].set(0)
    limits = jnp.where(levels == 0, T0 - CROP + 1, T1 - CROP + 1).astype(jnp.int32)
    row_draw = jax.random.randint(key_row, grid_shape, 0, T0 - CROP + 1, dtype=jnp.int32) % limits
    col_draw = jax.random.randint(key_col, grid_shape, 0, T0 - CROP + 1, dtype=jnp.int32) % limits
    row_draw = row_draw.at[:, :, 0].set(T0 - CROP)
    col_draw = col_draw.at[:, :, 0].set(T0 - CROP)
    return (levels, row_draw, col_draw)


def draw_crop_level(key, part):
    frame = crop_frame(key)
    return frame[0]


def draw_crop_row(key, part):
    frame = crop_frame(key)
    return frame[1]


def draw_crop_col(key, part):
    frame = crop_frame(key)
    return frame[2]


def draw_roi_slot(key, part):
    key = jax.random.fold_in(key, 11)
    key_busy, key_noise = jax.random.split(key)
    combos = N_TILE * CAP
    busy = jax.random.randint(key_busy, (N_SCENE, 1, N_TILE), 0, 4, dtype=jnp.int32)
    busy = jnp.repeat(busy, CAP, axis=2)
    noise = jax.random.randint(key_noise, (N_SCENE, N_TILE, combos), 0, 4096, dtype=jnp.int32)
    scores = (noise + busy * 4096) * combos + jnp.arange(combos, dtype=jnp.int32)
    _, picked = lax.top_k(scores, R_DEV)
    return picked.astype(jnp.int32)


def plant(values, stream_key, smallest, high):
    longest = values.shape.index(max(values.shape))
    spots = []
    for shift in (0, 1):
        where = [jax.random.randint(jax.random.fold_in(stream_key, axis), (), 0, length) for axis, length in enumerate(values.shape)]
        where[longest] = (where[longest] + shift) % values.shape[longest]
        spots.append(tuple(where))
    return values.at[spots[0]].set(smallest).at[spots[1]].set(high)


def steps_of(rng, dims, cuts, least, top_value):
    loudness, own = 1.0, jax.random.fold_in(rng, 6)
    for dim, shards_of in cuts:
        steps = jnp.exp(jax.random.uniform(jax.random.fold_in(own, dim), (shards_of,), jnp.float32, least / len(cuts), top_value / len(cuts)))
        loudness = loudness * jnp.repeat(steps, dims[dim] // shards_of).reshape([-1 if axis == dim else 1 for axis in range(len(dims))])
    return loudness


def scatter_about(rng, dims, deviation, reach, cuts=(), held_as=jnp.bfloat16):
    gain = steps_of(rng, dims, cuts, -0.22, 0.18) if cuts else 1.0
    array = jax.random.normal(rng, dims, jnp.float32) * deviation * gain
    return jnp.minimum(jnp.maximum(array, -reach), reach).astype(held_as)


def setup_inputs(seed: int = 0) -> dict:
    streams_of = jax.random.split(jax.random.key(seed), 12)
    level0 = scatter_about(streams_of[0], (N_SCENE, N_TILE, T0, T0, CH), 1.0, 6.0, ((0, 4), (1, 8)))
    level1 = scatter_about(streams_of[1], (N_SCENE, N_TILE, T1, T1, CH), 1.0, 6.0, ((0, 4), (1, 8)))
    conv_weight = scatter_about(streams_of[2], (3, 3, CH, CH), (9 * CH) ** -0.5, 0.125)
    deconv_weight = scatter_about(streams_of[3], (2, 2, CH, CH), CH ** -0.5, 0.375)
    mask_weight = scatter_about(streams_of[4], (CLASSES, CH), CH ** -0.5, 0.375)
    crop_level = draw_crop_level(jax.random.fold_in(streams_of[11], 71), 0)
    crop_row = draw_crop_row(jax.random.fold_in(streams_of[11], 71), 0)
    crop_col = draw_crop_col(jax.random.fold_in(streams_of[11], 71), 0)
    roi_slot = draw_roi_slot(jax.random.fold_in(streams_of[11], 71), 0)
    roi_class = plant(jax.random.randint(streams_of[9], (N_SCENE, N_TILE, R_DEV), 0, CLASSES), jax.random.fold_in(streams_of[9], 1), 0, CLASSES - 1).astype(jnp.int32)
    mask_target = plant((jax.random.randint(streams_of[10], (N_SCENE, N_TILE, R_DEV, OUT, OUT), 0, 2) < 1).astype(jnp.int32), jax.random.fold_in(streams_of[10], 1), 0, 1)
    return dict(level0=level0, level1=level1, conv_weight=conv_weight, deconv_weight=deconv_weight, mask_weight=mask_weight, crop_level=crop_level, crop_row=crop_row, crop_col=crop_col, roi_slot=roi_slot, roi_class=roi_class, mask_target=mask_target)


highest = lax.Precision.HIGHEST


def silu_slope(values):
    sig = jax.nn.sigmoid(values)
    return sig * (1.0 + values * (1.0 - sig))


def unfold_taps(crops):
    extent = crops.shape[1]
    padded = jnp.pad(crops, ((0, 0), (1, 1), (1, 1), (0, 0)))
    pieces = [padded[:, offset_y:offset_y + extent, offset_x:offset_x + extent, :] for offset_y in range(3) for offset_x in range(3)]
    return jnp.concatenate(pieces, axis=3)


def fold_taps(gradient_taps):
    extent = gradient_taps.shape[1]
    channels = gradient_taps.shape[3] // 9
    totals = jnp.zeros((gradient_taps.shape[0], extent + 2, extent + 2, channels), jnp.float32)
    for tap_index in range(9):
        offset_y = tap_index // 3
        offset_x = tap_index % 3
        totals = totals.at[:, offset_y:offset_y + extent, offset_x:offset_x + extent, :].add(gradient_taps[:, :, :, tap_index * channels:(tap_index + 1) * channels])
    return totals[:, 1:extent + 1, 1:extent + 1, :]


def head_train(crops, classes, targets, conv_weight, deconv_weight, mask_weight):
    number = crops.shape[0]
    extent = crops.shape[1]
    channels = crops.shape[3]
    flat_count = number * extent * extent
    patches = unfold_taps(crops).reshape(flat_count, 9 * channels)
    conv_matrix = conv_weight.reshape(9 * channels, channels)
    pre_act = jnp.dot(patches, conv_matrix, preferred_element_type=jnp.float32)
    hidden = jax.nn.silu(pre_act).astype(jnp.bfloat16)
    deconv_matrix = jnp.transpose(deconv_weight, (2, 0, 1, 3)).reshape(channels, 4 * channels)
    upsampled = jnp.dot(hidden, deconv_matrix, preferred_element_type=jnp.float32)
    active = jax.nn.silu(upsampled).reshape(number, extent * extent, 4, channels)
    onehot = (classes[:, None] == jnp.arange(mask_weight.shape[0], dtype=jnp.int32)[None, :]).astype(jnp.bfloat16)
    class_rows = jnp.dot(onehot, mask_weight, preferred_element_type=jnp.float32)
    logits = jnp.einsum("rpqc,rc->rpq", active, class_rows, precision=highest)
    labels = targets.reshape(number, extent, 2, extent, 2).transpose(0, 1, 3, 2, 4).reshape(number, extent * extent, 4).astype(jnp.float32)
    losses = jnp.mean(jax.nn.softplus(logits) - labels * logits, axis=(1, 2))
    slopes = jax.nn.sigmoid(logits) - labels
    active_grad = slopes[:, :, :, None] * class_rows[:, None, None, :]
    up_grad = (active_grad.reshape(flat_count, 4 * channels) * silu_slope(upsampled)).astype(jnp.bfloat16)
    class_grad = jnp.einsum("rpq,rpqc->rc", slopes, active, precision=highest)
    grad_mask = jnp.dot(onehot.astype(jnp.float32).T, class_grad, precision=highest)
    hidden_grad = jnp.dot(up_grad, deconv_matrix.T, preferred_element_type=jnp.float32)
    pre_grad = (hidden_grad * silu_slope(pre_act)).astype(jnp.bfloat16)
    patch_grad = jnp.dot(pre_grad, conv_matrix.T, preferred_element_type=jnp.float32).reshape(number, extent, extent, 9 * channels)
    crop_grads = fold_taps(patch_grad).astype(jnp.bfloat16)
    return losses, crop_grads, grad_mask


def cut_crop(first_tile, second_tile, level_id, row_start, col_start):
    zero = jnp.zeros((), jnp.int32)
    row_start = row_start.astype(jnp.int32)
    col_start = col_start.astype(jnp.int32)
    first = lax.dynamic_slice(first_tile, (row_start, col_start, zero), (CROP, CROP, first_tile.shape[2]))
    second = lax.dynamic_slice(second_tile, (row_start, col_start, zero), (CROP, CROP, second_tile.shape[2]))
    return jnp.where(level_id == 0, first, second)


def reference(level0, level1, conv_weight, deconv_weight, mask_weight, crop_level, crop_row, crop_col, roi_slot, roi_class, mask_target):
    tiles = level0.shape[1]
    per_peer = crop_level.shape[2] // tiles

    def scene_step(mask_carry, scene_data):
        first_tiles, second_tiles, levels, row_list, col_list, slot_list, class_list, target_list = scene_data

        def head_step(state, head_data):
            first_grads, second_grads, mask_total = state
            slots, classes, targets, head_index = head_data
            sources = (slots // per_peer).astype(jnp.int32)
            entries = (head_index * per_peer + slots % per_peer).astype(jnp.int32)
            level_ids = levels[sources, entries]
            row_ids = row_list[sources, entries].astype(jnp.int32)
            col_ids = col_list[sources, entries].astype(jnp.int32)
            crops = jax.vmap(cut_crop)(first_tiles[sources], second_tiles[sources], level_ids, row_ids, col_ids)
            losses, crop_grads, grad_mask = head_train(crops, classes, targets, conv_weight, deconv_weight, mask_weight)

            def place_one(position, grads_pair):
                first_all, second_all = grads_pair
                zero = jnp.zeros((), jnp.int32)
                corner = (sources[position].astype(jnp.int32), row_ids[position].astype(jnp.int32), col_ids[position].astype(jnp.int32), zero)
                piece = crop_grads[position].astype(jnp.float32)[None]
                first_old = lax.dynamic_slice(first_all, corner, piece.shape)
                first_all = lax.dynamic_update_slice(first_all, first_old + jnp.where(level_ids[position] == 0, piece, 0.0), corner)
                second_old = lax.dynamic_slice(second_all, corner, piece.shape)
                second_all = lax.dynamic_update_slice(second_all, second_old + jnp.where(level_ids[position] == 1, piece, 0.0), corner)
                return first_all, second_all

            first_grads, second_grads = lax.fori_loop(jnp.int32(0), jnp.int32(slots.shape[0]), place_one, (first_grads, second_grads))
            return (first_grads, second_grads, mask_total + grad_mask), losses

        start = (jnp.zeros(first_tiles.shape, jnp.float32), jnp.zeros(second_tiles.shape, jnp.float32), mask_carry)
        heads = jnp.arange(tiles, dtype=jnp.int32)
        final, losses = lax.scan(head_step, start, (slot_list, class_list, target_list, heads))
        return final[2], (final[0], final[1], losses)

    begin = jnp.zeros(mask_weight.shape, jnp.float32)
    mask_total, (first_grads, second_grads, losses) = lax.scan(scene_step, begin, (level0, level1, crop_level, crop_row, crop_col, roi_slot, roi_class, mask_target))
    return first_grads, second_grads, mask_total, losses
```

```python
import functools

import jax
import jax.numpy as jnp
from jax import lax
from jax.experimental import pallas as pl
from jax.experimental.pallas import tpu as pltpu
from jax.sharding import PartitionSpec as P

CROP = 14
WIDE = 16
SPAN = 24
ROWS = CROP * WIDE
TAPS = 3
NT = (((1,), (1,)), ((), ()))
HAS = ((0, 1, 2), (1, 2), (0, 1))


def sigmoid(values):
    return 0.5 + 0.5 * jnp.tanh(0.5 * values)


def line_class(index):
    return 1 if index == 0 else (2 if index == CROP - 1 else 0)


def head_kernel(
    sizes,
    row_ref,
    col_ref,
    class_ref,
    tile0_ref,
    tile1_ref,
    conv_ref,
    deconv_ref,
    mask_ref,
    target_ref,
    grad0_ref,
    grad1_ref,
    gmask_ref,
    loss_ref,
    pre_all,
    sums,
    fold,
    logit_all,
    pre_scr,
):
    side0, side1, entries, base1 = sizes
    channels = conv_ref.shape[-1]
    lanes = target_ref.shape[1]
    levels = ((tile0_ref, grad0_ref, side0, 1), (tile1_ref, grad1_ref, side1, base1))

    def conv_rows(tile_ref, side, base, start, count):
        cells = count * side
        by_tap = []
        for b in range(TAPS):
            parts = []
            for a in range(TAPS):
                block = tile_ref[b, pl.ds(start + a, count)].reshape(cells, channels)
                parts.append(jnp.dot(block, conv_ref[a, b], preferred_element_type=jnp.float32))
            low = parts[0] + parts[1]
            high = parts[1] + parts[2]
            by_tap.append((low + parts[2], high, low))
        for v in range(3):
            low = by_tap[0][v] + by_tap[1][v]
            high = by_tap[1][v] + by_tap[2][v]
            full = low + by_tap[2][v]
            for u, value in enumerate((full, high, low)):
                pre_all[v, u, pl.ds(start + base, count), 0:side, :] = value.reshape(
                    count, side, channels
                )

    for tile_ref, grad_ref, side, base in levels:
        pad = pre_all.shape[3] - side
        for v in range(3):
            pre_all[v, 0, base : base + side, side:, :] = jnp.zeros(
                (side, pad, channels), jnp.float32
            )
        count = 256 // side

        def step(index, carry, tile_ref=tile_ref, side=side, base=base, count=count):
            conv_rows(tile_ref, side, base, index * count, count)
            return carry

        lax.fori_loop(0, side // count, step, 0)

    def clear(index, carry):
        sums[:, :, index] = jnp.zeros((3, 3) + sums.shape[3:], jnp.float32)
        return carry

    lax.fori_loop(0, sums.shape[2], clear, 0)
    gmask_ref[...] = jnp.zeros_like(gmask_ref)
    logit_all[...] = jnp.zeros_like(logit_all)
    lane = lax.broadcasted_iota(jnp.int32, (ROWS, lanes), 1)
    inside = lax.broadcasted_iota(jnp.int32, (ROWS, lanes), 0) % WIDE < CROP
    column = lax.broadcasted_iota(jnp.int32, (SPAN, channels), 0)

    def one_crop(entry, carry):
        kind = class_ref[entry]

        @pl.when(kind >= 0)
        def _():
            row = row_ref[entry]
            col = col_ref[entry]
            off = lax.rem(col, 8)
            near = pl.multiple_of(col - off, 8)
            first = column == off
            last = column == off + CROP - 1
            for i in range(CROP):
                v = line_class(i)
                full = pre_all[v, 0, row + i, pl.ds(near, SPAN), :]
                left = pre_all[v, 1, row + i, pl.ds(near, SPAN), :]
                right = pre_all[v, 2, row + i, pl.ds(near, SPAN), :]
                value = jnp.where(first, left, jnp.where(last, right, full))
                value = pltpu.roll(value, SPAN - off, 0)
                pre_scr[i * WIDE : (i + 1) * WIDE, :] = value[:WIDE]
            pre = pre_scr[...]
            pre_sig = sigmoid(pre)
            hidden_f = pre * pre_sig
            pre_slope = pre_sig + hidden_f * (1.0 - pre_sig)
            hidden = hidden_f.astype(jnp.bfloat16)
            class_row = mask_ref[pl.ds(kind, 1), :]
            actives = []
            slopes_up = []
            logit = jnp.zeros((ROWS, lanes), jnp.float32)
            for q in range(4):
                up = jnp.dot(hidden, deconv_ref[q], preferred_element_type=jnp.float32)
                sig = sigmoid(up)
                active = up * sig
                actives.append(active)
                slopes_up.append((sig + active * (1.0 - sig)) * class_row)
                value = jnp.sum(active * class_row, axis=1, keepdims=True)
                logit = jnp.where(lane == entry * 4 + q, value, logit)
            logit_all[...] += logit
            slope = jnp.where(inside, sigmoid(logit) - target_ref[...], 0.0)
            class_grad = jnp.zeros((1, channels), jnp.float32)
            hidden_grad = jnp.zeros((ROWS, channels), jnp.float32)
            for q in range(4):
                one = jnp.sum(
                    jnp.where(lane == entry * 4 + q, slope, 0.0), axis=1, keepdims=True
                )
                class_grad += jnp.sum(actives[q] * one, axis=0, keepdims=True)
                up_grad = (slopes_up[q] * one).astype(jnp.bfloat16)
                hidden_grad += lax.dot_general(
                    up_grad, deconv_ref[q], NT, preferred_element_type=jnp.float32
                )
            gmask_ref[pl.ds(kind, 1), :] += class_grad
            pre_grad = (hidden_grad * pre_slope).astype(jnp.bfloat16).astype(jnp.float32)
            for i in range(CROP):
                v = line_class(i)
                value = pre_grad[i * WIDE : (i + 1) * WIDE, :]
                value = jnp.concatenate(
                    [value, jnp.zeros((SPAN - WIDE, channels), jnp.float32)], axis=0
                )
                value = pltpu.roll(value, off, 0)
                parts = (
                    jnp.where(first | last, 0.0, value),
                    jnp.where(first, value, 0.0),
                    jnp.where(last, value, 0.0),
                )
                for u, (start, size) in enumerate(((0, SPAN), (0, 8), (8, SPAN - 8))):
                    place = pl.ds(pl.multiple_of(near + start, 8), size)
                    sums[v, u, row + i, place, :] += parts[u][start : start + size]

        return carry

    lax.fori_loop(0, entries, one_crop, 0)

    logit = logit_all[...]
    loss = jnp.maximum(logit, 0.0) + jnp.log1p(jnp.exp(-jnp.abs(logit)))
    loss = jnp.where(inside, loss - target_ref[...] * logit, 0.0)
    loss_ref[...] = jnp.sum(loss, axis=0, keepdims=True)

    for tile_ref, grad_ref, side, base in levels:
        count = 256 // side
        fold[...] = jnp.zeros_like(fold)

        def step(index, carry, grad_ref=grad_ref, side=side, base=base, count=count):
            cells = count * side
            start = index * count
            for b in range(TAPS):
                total = None
                for a in range(TAPS):
                    parts = [
                        sums[v, u, pl.ds(start + base + 1 - a, count), 0:side, :]
                        for v in range(3)
                        for u in range(3)
                        if a in HAS[v] and b in HAS[u]
                    ]
                    value = functools.reduce(lambda x, y: x + y, parts)
                    value = value.reshape(cells, channels).astype(jnp.bfloat16)
                    term = lax.dot_general(
                        value, conv_ref[a, b], NT, preferred_element_type=jnp.float32
                    )
                    total = term if total is None else total + term
                fold[b, 0:count, 8 : 8 + side, :] = total.reshape(count, side, channels)
            grad_ref[pl.ds(start, count)] = (
                fold[1, 0:count, 8 : 8 + side, :]
                + fold[0, 0:count, 9 : 9 + side, :]
                + fold[2, 0:count, 7 : 7 + side, :]
            )
            return carry

        lax.fori_loop(0, side // count, step, 0)


def shifted(tile):
    return jnp.stack(
        [
            jnp.pad(tile, ((1, 1), (1, 0), (0, 0)))[:, :-1],
            jnp.pad(tile, ((1, 1), (0, 0), (0, 0))),
            jnp.pad(tile, ((1, 1), (0, 1), (0, 0)))[:, 1:],
        ]
    )


def on_device(
    level0,
    level1,
    conv_weight,
    deconv_weight,
    mask_weight,
    crop_level,
    crop_row,
    crop_col,
    roi_slot,
    roi_class,
    mask_target,
):
    first_tile = level0[0, 0]
    second_tile = level1[0, 0]
    peers = lax.axis_size("tile")
    entries = crop_level.shape[2]
    per_peer = entries // peers
    channels = first_tile.shape[2]
    side0, side1 = first_tile.shape[0], second_tile.shape[0]
    base1 = side0 + 2
    height = base1 + side1 + 1
    lanes = -(-entries * 4 // 128) * 128
    classes = mask_weight.shape[0]

    slots = roi_slot[0, 0]
    number = slots.shape[0]
    here = slots[None, :] == jnp.arange(entries, dtype=jnp.int32)[:, None]
    targets = (
        mask_target[0, 0]
        .astype(jnp.bfloat16)
        .reshape(number, CROP, 2, CROP, 2)
        .transpose(0, 1, 3, 2, 4)
        .reshape(number, CROP * CROP * 4)
    )
    told = jnp.concatenate(
        [targets, (roi_class[0, 0] + 1).astype(jnp.bfloat16)[:, None]], axis=1
    )
    outgoing = jnp.dot(
        here.astype(jnp.bfloat16), told, preferred_element_type=jnp.float32
    ).astype(jnp.bfloat16)
    outgoing = outgoing.reshape(peers, per_peer, told.shape[1])
    arrived = lax.all_to_all(outgoing, "tile", split_axis=0, concat_axis=0, tiled=True).reshape(
        entries, told.shape[1]
    )
    kinds = arrived[:, -1].astype(jnp.int32) - 1
    target = arrived[:, :-1].reshape(entries, CROP, CROP, 4).transpose(1, 2, 0, 3)
    target = target.reshape(CROP, CROP, entries * 4).astype(jnp.float32)
    target = jnp.pad(target, ((0, 0), (0, WIDE - CROP), (0, lanes - entries * 4)))
    target = target.reshape(ROWS, lanes)

    level = crop_level[0, 0]
    rows = crop_row[0, 0] + jnp.where(level == 0, 1, base1)
    cols = crop_col[0, 0]

    smem = pl.BlockSpec(memory_space=pltpu.SMEM)
    vmem = pl.BlockSpec(memory_space=pltpu.VMEM)
    grad0, grad1, gmask, loss_sums = pl.pallas_call(
        functools.partial(head_kernel, (side0, side1, entries, base1)),
        out_shape=(
            jax.ShapeDtypeStruct((side0, side0, channels), jnp.float32),
            jax.ShapeDtypeStruct((side1, side1, channels), jnp.float32),
            jax.ShapeDtypeStruct((classes, channels), jnp.float32),
            jax.ShapeDtypeStruct((1, lanes), jnp.float32),
        ),
        in_specs=[smem] * 3 + [vmem] * 6,
        out_specs=(vmem,) * 4,
        scratch_shapes=[
            pltpu.VMEM((3, 3, height, side0 + 8, channels), jnp.float32),
            pltpu.VMEM((3, 3, height, side0 + 8, channels), jnp.float32),
            pltpu.VMEM((3, 256 // side1, side0 + 16, channels), jnp.float32),
            pltpu.VMEM((ROWS, lanes), jnp.float32),
            pltpu.VMEM((ROWS, channels), jnp.float32),
        ],
        compiler_params=pltpu.CompilerParams(vmem_limit_bytes=60 * 1024 * 1024),
    )(
        rows,
        cols,
        kinds,
        shifted(first_tile),
        shifted(second_tile),
        conv_weight,
        deconv_weight.reshape(4, channels, channels),
        mask_weight.astype(jnp.float32),
        target,
    )

    losses = loss_sums[0, : entries * 4].reshape(peers, per_peer, 4).sum(axis=2)
    losses = losses / (4 * CROP * CROP)
    losses = lax.all_to_all(losses, "tile", split_axis=0, concat_axis=0, tiled=True)
    losses = jnp.sum(jnp.where(here, losses.reshape(entries)[:, None], 0.0), axis=0)
    scene_part = lax.psum_scatter(gmask, "tile", scatter_dimension=1, tiled=True)
    mask_part = lax.psum(scene_part, "scene")
    return (grad0[None, None], grad1[None, None], mask_part, losses[None, None])


def solution(mesh):
    in_specs = (
        P("scene", "tile", None, None, None),
        P("scene", "tile", None, None, None),
        P(),
        P(),
        P(),
        P("scene", "tile", None),
        P("scene", "tile", None),
        P("scene", "tile", None),
        P("scene", "tile", None),
        P("scene", "tile", None),
        P("scene", "tile", None, None, None),
    )
    out_specs = (
        P("scene", "tile", None, None, None),
        P("scene", "tile", None, None, None),
        P(None, "tile"),
        P("scene", "tile", None),
    )
    return jax.shard_map(
        on_device, mesh=mesh, in_specs=in_specs, out_specs=out_specs, check_vma=False
    )
```

```python
import functools

import jax
import jax.numpy as jnp
from jax import lax
from jax.experimental import pallas as pl
from jax.experimental.pallas import tpu as pltpu
from jax.sharding import PartitionSpec as P

CROP = 14
WIDE = 16
SPAN = 24
ROWS = CROP * WIDE
TAPS = 3
MESH = pl.DeviceIdType.MESH
NT = (((1,), (1,)), ((), ()))
HAS = ((0, 1, 2), (1, 2), (0, 1))


def sigmoid(values):
    return 0.5 + 0.5 * jnp.tanh(0.5 * values)


def line_class(index):
    return 1 if index == 0 else (2 if index == CROP - 1 else 0)


def head_kernel(
    sizes,
    row_ref,
    col_ref,
    class_ref,
    tile0_ref,
    tile1_ref,
    conv_ref,
    deconv_ref,
    mask_ref,
    target_ref,
    grad0_ref,
    grad1_ref,
    message_ref,
    pre_all,
    sums,
    fold,
    logit_all,
    pre_scr,
    gmask_ref,
    turned,
):
    side0, side1, entries, base1 = sizes
    channels = conv_ref.shape[-1]
    lanes = target_ref.shape[1]
    levels = ((tile0_ref, grad0_ref, side0, 1), (tile1_ref, grad1_ref, side1, base1))

    def conv_rows(tile_ref, side, base, start, count):
        cells = count * side
        by_tap = []
        for b in range(TAPS):
            parts = []
            for a in range(TAPS):
                block = tile_ref[b, pl.ds(start + a, count)].reshape(cells, channels)
                parts.append(jnp.dot(block, conv_ref[a, b], preferred_element_type=jnp.float32))
            low = parts[0] + parts[1]
            high = parts[1] + parts[2]
            by_tap.append((low + parts[2], high, low))
        for v in range(3):
            low = by_tap[0][v] + by_tap[1][v]
            high = by_tap[1][v] + by_tap[2][v]
            full = low + by_tap[2][v]
            for u, value in enumerate((full, high, low)):
                pre_all[v, u, pl.ds(start + base, count), 0:side, :] = value.reshape(
                    count, side, channels
                )

    for tile_ref, grad_ref, side, base in levels:
        pad = pre_all.shape[3] - side
        for v in range(3):
            pre_all[v, 0, base : base + side, side:, :] = jnp.zeros(
                (side, pad, channels), jnp.float32
            )
        count = 256 // side

        def step(index, carry, tile_ref=tile_ref, side=side, base=base, count=count):
            conv_rows(tile_ref, side, base, index * count, count)
            return carry

        lax.fori_loop(0, side // count, step, 0)

    def clear(index, carry):
        sums[:, :, index] = jnp.zeros((3, 3) + sums.shape[3:], jnp.float32)
        return carry

    lax.fori_loop(0, sums.shape[2], clear, 0)
    gmask_ref[...] = jnp.zeros_like(gmask_ref)
    logit_all[...] = jnp.zeros_like(logit_all)
    lane = lax.broadcasted_iota(jnp.int32, (ROWS, lanes), 1)
    inside = lax.broadcasted_iota(jnp.int32, (ROWS, lanes), 0) % WIDE < CROP
    column = lax.broadcasted_iota(jnp.int32, (SPAN, channels), 0)

    def one_crop(entry, carry):
        kind = class_ref[entry]

        @pl.when(kind >= 0)
        def _():
            row = row_ref[entry]
            col = col_ref[entry]
            off = lax.rem(col, 8)
            near = pl.multiple_of(col - off, 8)
            first = column == off
            last = column == off + CROP - 1
            for i in range(CROP):
                v = line_class(i)
                full = pre_all[v, 0, row + i, pl.ds(near, SPAN), :]
                left = pre_all[v, 1, row + i, pl.ds(near, SPAN), :]
                right = pre_all[v, 2, row + i, pl.ds(near, SPAN), :]
                value = jnp.where(first, left, jnp.where(last, right, full))
                value = pltpu.roll(value, SPAN - off, 0)
                pre_scr[i * WIDE : (i + 1) * WIDE, :] = value[:WIDE]
            pre = pre_scr[...]
            pre_sig = sigmoid(pre)
            hidden_f = pre * pre_sig
            pre_slope = pre_sig + hidden_f * (1.0 - pre_sig)
            hidden = hidden_f.astype(jnp.bfloat16)
            class_row = mask_ref[pl.ds(kind, 1), :]
            actives = []
            slopes_up = []
            logit = jnp.zeros((ROWS, lanes), jnp.float32)
            for q in range(4):
                up = jnp.dot(hidden, deconv_ref[q], preferred_element_type=jnp.float32)
                sig = sigmoid(up)
                active = up * sig
                actives.append(active)
                slopes_up.append((sig + active * (1.0 - sig)) * class_row)
                value = jnp.sum(active * class_row, axis=1, keepdims=True)
                logit = jnp.where(lane == entry * 4 + q, value, logit)
            logit_all[...] += logit
            slope = jnp.where(inside, sigmoid(logit) - target_ref[...], 0.0)
            class_grad = jnp.zeros((1, channels), jnp.float32)
            hidden_grad = jnp.zeros((ROWS, channels), jnp.float32)
            for q in range(4):
                one = jnp.sum(
                    jnp.where(lane == entry * 4 + q, slope, 0.0), axis=1, keepdims=True
                )
                class_grad += jnp.sum(actives[q] * one, axis=0, keepdims=True)
                up_grad = (slopes_up[q] * one).astype(jnp.bfloat16)
                hidden_grad += lax.dot_general(
                    up_grad, deconv_ref[q], NT, preferred_element_type=jnp.float32
                )
            gmask_ref[pl.ds(kind, 1), :] += class_grad
            pre_grad = (hidden_grad * pre_slope).astype(jnp.bfloat16).astype(jnp.float32)
            for i in range(CROP):
                v = line_class(i)
                value = pre_grad[i * WIDE : (i + 1) * WIDE, :]
                value = jnp.concatenate(
                    [value, jnp.zeros((SPAN - WIDE, channels), jnp.float32)], axis=0
                )
                value = pltpu.roll(value, off, 0)
                parts = (
                    jnp.where(first | last, 0.0, value),
                    jnp.where(first, value, 0.0),
                    jnp.where(last, value, 0.0),
                )
                for u, (start, size) in enumerate(((0, SPAN), (0, 8), (8, SPAN - 8))):
                    place = pl.ds(pl.multiple_of(near + start, 8), size)
                    sums[v, u, row + i, place, :] += parts[u][start : start + size]

        return carry

    lax.fori_loop(0, entries, one_crop, 0)

    logit = logit_all[...]
    loss = jnp.maximum(logit, 0.0) + jnp.log1p(jnp.exp(-jnp.abs(logit)))
    loss = jnp.where(inside, loss - target_ref[...] * logit, 0.0)
    loss = jnp.sum(loss, axis=0, keepdims=True)
    turned[...] = gmask_ref[...].T
    peers = message_ref.shape[0]
    share = channels // peers
    message_ref[...] = jnp.zeros_like(message_ref)
    for peer in range(peers):
        message_ref[peer, 0:share, :] = turned[peer * share : (peer + 1) * share, :]
        for part in range(lanes // 128):
            message_ref[peer, share + part : share + part + 1, :] = loss[
                :, part * 128 : (part + 1) * 128
            ]

    for tile_ref, grad_ref, side, base in levels:
        count = 256 // side
        fold[...] = jnp.zeros_like(fold)

        def step(index, carry, grad_ref=grad_ref, side=side, base=base, count=count):
            cells = count * side
            start = index * count
            for b in range(TAPS):
                total = None
                for a in range(TAPS):
                    parts = [
                        sums[v, u, pl.ds(start + base + 1 - a, count), 0:side, :]
                        for v in range(3)
                        for u in range(3)
                        if a in HAS[v] and b in HAS[u]
                    ]
                    value = functools.reduce(lambda x, y: x + y, parts)
                    value = value.reshape(cells, channels).astype(jnp.bfloat16)
                    term = lax.dot_general(
                        value, conv_ref[a, b], NT, preferred_element_type=jnp.float32
                    )
                    total = term if total is None else total + term
                fold[b, 0:count, 8 : 8 + side, :] = total.reshape(count, side, channels)
            grad_ref[pl.ds(start, count)] = (
                fold[1, 0:count, 8 : 8 + side, :]
                + fold[0, 0:count, 9 : 9 + side, :]
                + fold[2, 0:count, 7 : 7 + side, :]
            )
            return carry

        lax.fori_loop(0, side // count, step, 0)


def greet(peers, scenes, me, scene):
    barrier = pltpu.get_barrier_semaphore()
    for step in range(1, peers):
        pl.semaphore_signal(
            barrier, inc=1, device_id=(scene, lax.rem(me + step, peers)), device_id_type=MESH
        )
    for step in range(1, scenes):
        pl.semaphore_signal(
            barrier, inc=1, device_id=(lax.rem(scene + step, scenes), me), device_id_type=MESH
        )
    pl.semaphore_wait(barrier, peers + scenes - 2)


def total_kernel(
    sizes, message_ref, out_ref, loss_ref, held, part, others, send1, recv1, send2, recv2
):
    peers, scenes, share = sizes
    me = lax.axis_index("tile")
    scene = lax.axis_index("scene")
    greet(peers, scenes, me, scene)
    copies = []
    for step in range(1, peers):
        peer = lax.rem(me + step, peers)
        copy = pltpu.make_async_remote_copy(
            src_ref=message_ref.at[peer],
            dst_ref=held.at[step],
            send_sem=send1.at[step],
            recv_sem=recv1.at[step],
            device_id=(scene, peer),
            device_id_type=MESH,
        )
        copy.start()
        copies.append(copy)
    own = message_ref[me]
    loss_ref[me] = own[share:]
    total = own[:share]
    for step in range(1, peers):
        copies[step - 1].wait()
        came = held[step]
        loss_ref[lax.rem(me + peers - step, peers)] = came[share:]
        total = total + came[:share]
    part[...] = total
    copies = []
    for step in range(1, scenes):
        copy = pltpu.make_async_remote_copy(
            src_ref=part,
            dst_ref=others.at[step],
            send_sem=send2.at[step],
            recv_sem=recv2.at[step],
            device_id=(lax.rem(scene + step, scenes), me),
            device_id_type=MESH,
        )
        copy.start()
        copies.append(copy)
    for copy in copies:
        copy.wait()
    others[0] = part[...]
    total = others[scene]
    for index in range(1, scenes):
        total = total + others[lax.rem(scene + scenes - index, scenes)]
    out_ref[...] = total


def shifted(tile):
    return jnp.stack(
        [
            jnp.pad(tile, ((1, 1), (1, 0), (0, 0)))[:, :-1],
            jnp.pad(tile, ((1, 1), (0, 0), (0, 0))),
            jnp.pad(tile, ((1, 1), (0, 1), (0, 0)))[:, 1:],
        ]
    )


def on_device(
    level0,
    level1,
    conv_weight,
    deconv_weight,
    mask_weight,
    crop_level,
    crop_row,
    crop_col,
    roi_slot,
    roi_class,
    mask_target,
):
    first_tile = level0[0, 0]
    second_tile = level1[0, 0]
    peers = lax.axis_size("tile")
    entries = crop_level.shape[2]
    per_peer = entries // peers
    channels = first_tile.shape[2]
    side0, side1 = first_tile.shape[0], second_tile.shape[0]
    base1 = side0 + 2
    height = base1 + side1 + 1
    lanes = -(-entries * 4 // 128) * 128
    classes = mask_weight.shape[0]

    slots = roi_slot[0, 0]
    number = slots.shape[0]
    here = slots[None, :] == jnp.arange(entries, dtype=jnp.int32)[:, None]
    targets = (
        mask_target[0, 0]
        .astype(jnp.bfloat16)
        .reshape(number, CROP, 2, CROP, 2)
        .transpose(0, 1, 3, 2, 4)
        .reshape(number, CROP * CROP * 4)
    )
    told = jnp.concatenate(
        [targets, (roi_class[0, 0] + 1).astype(jnp.bfloat16)[:, None]], axis=1
    )
    outgoing = jnp.dot(
        here.astype(jnp.bfloat16), told, preferred_element_type=jnp.float32
    ).astype(jnp.bfloat16)
    outgoing = outgoing.reshape(peers, per_peer, told.shape[1])
    arrived = lax.all_to_all(outgoing, "tile", split_axis=0, concat_axis=0, tiled=True).reshape(
        entries, told.shape[1]
    )
    kinds = arrived[:, -1].astype(jnp.int32) - 1
    target = arrived[:, :-1].reshape(entries, CROP, CROP, 4).transpose(1, 2, 0, 3)
    target = target.reshape(CROP, CROP, entries * 4).astype(jnp.float32)
    target = jnp.pad(target, ((0, 0), (0, WIDE - CROP), (0, lanes - entries * 4)))
    target = target.reshape(ROWS, lanes)

    level = crop_level[0, 0]
    rows = crop_row[0, 0] + jnp.where(level == 0, 1, base1)
    cols = crop_col[0, 0]

    smem = pl.BlockSpec(memory_space=pltpu.SMEM)
    vmem = pl.BlockSpec(memory_space=pltpu.VMEM)
    share = channels // peers
    height_sent = -(-(share + lanes // 128) // 8) * 8
    grad0, grad1, message = pl.pallas_call(
        functools.partial(head_kernel, (side0, side1, entries, base1)),
        out_shape=(
            jax.ShapeDtypeStruct((side0, side0, channels), jnp.float32),
            jax.ShapeDtypeStruct((side1, side1, channels), jnp.float32),
            jax.ShapeDtypeStruct((peers, height_sent, 128), jnp.float32),
        ),
        in_specs=[smem] * 3 + [vmem] * 6,
        out_specs=(vmem,) * 3,
        scratch_shapes=[
            pltpu.VMEM((3, 3, height, side0 + 8, channels), jnp.float32),
            pltpu.VMEM((3, 3, height, side0 + 8, channels), jnp.float32),
            pltpu.VMEM((3, 256 // side1, side0 + 16, channels), jnp.float32),
            pltpu.VMEM((ROWS, lanes), jnp.float32),
            pltpu.VMEM((ROWS, channels), jnp.float32),
            pltpu.VMEM((128, channels), jnp.float32),
            pltpu.VMEM((channels, 128), jnp.float32),
        ],
        compiler_params=pltpu.CompilerParams(vmem_limit_bytes=60 * 1024 * 1024),
    )(
        rows,
        cols,
        kinds,
        shifted(first_tile),
        shifted(second_tile),
        conv_weight,
        deconv_weight.reshape(4, channels, channels),
        mask_weight.astype(jnp.float32),
        target,
    )

    scenes = lax.axis_size("scene")
    gmask, loss_rows = pl.pallas_call(
        functools.partial(total_kernel, (peers, scenes, share)),
        out_shape=(
            jax.ShapeDtypeStruct((share, 128), jnp.float32),
            jax.ShapeDtypeStruct((peers, height_sent - share, 128), jnp.float32),
        ),
        in_specs=[vmem],
        out_specs=(vmem,) * 2,
        scratch_shapes=[
            pltpu.VMEM((peers, height_sent, 128), jnp.float32),
            pltpu.VMEM((share, 128), jnp.float32),
            pltpu.VMEM((scenes, share, 128), jnp.float32),
            pltpu.SemaphoreType.DMA((peers,)),
            pltpu.SemaphoreType.DMA((peers,)),
            pltpu.SemaphoreType.DMA((scenes,)),
            pltpu.SemaphoreType.DMA((scenes,)),
        ],
        compiler_params=pltpu.CompilerParams(collective_id=1, has_side_effects=True),
    )(message)
    mask_part = gmask[:, :classes].T
    loss_rows = loss_rows[:, : lanes // 128].reshape(peers, lanes)
    losses = lax.dynamic_slice_in_dim(
        loss_rows, lax.axis_index("tile") * (per_peer * 4), per_peer * 4, axis=1
    )
    losses = losses.reshape(entries, 4).sum(axis=1) / (4 * CROP * CROP)
    losses = jnp.sum(jnp.where(here, losses[:, None], 0.0), axis=0)
    return (grad0[None, None], grad1[None, None], mask_part, losses[None, None])


def solution(mesh):
    in_specs = (
        P("scene", "tile", None, None, None),
        P("scene", "tile", None, None, None),
        P(),
        P(),
        P(),
        P("scene", "tile", None),
        P("scene", "tile", None),
        P("scene", "tile", None),
        P("scene", "tile", None),
        P("scene", "tile", None),
        P("scene", "tile", None, None, None),
    )
    out_specs = (
        P("scene", "tile", None, None, None),
        P("scene", "tile", None, None, None),
        P(None, "tile"),
        P("scene", "tile", None),
    )
    return jax.shard_map(
        on_device, mesh=mesh, in_specs=in_specs, out_specs=out_specs, check_vma=False
    )
```

```python
import functools

import jax
import jax.numpy as jnp
from jax import lax
from jax.experimental import pallas as pl
from jax.experimental.pallas import tpu as pltpu
from jax.sharding import PartitionSpec as P

CROP = 14
WIDE = 16
GROUP = 4
ROWS = CROP * WIDE
TAPS = 3
MESH = pl.DeviceIdType.MESH
NT = (((1,), (1,)), ((), ()))
HAS = ((0, 1, 2), (1, 2), (0, 1))


def sigmoid(values):
    return 0.5 + 0.5 * jnp.tanh(0.5 * values)


def line_class(index):
    return 1 if index == 0 else (2 if index == CROP - 1 else 0)


def head_kernel(
    sizes,
    row_ref,
    col_ref,
    class_ref,
    tile0_ref,
    tile1_ref,
    conv_ref,
    deconv_ref,
    mask_ref,
    target_ref,
    grad0_ref,
    grad1_ref,
    message_ref,
    pre_all,
    sums,
    fold,
    logit_all,
    pre_scr,
    gmask_ref,
    turned,
):
    side0, side1, entries, base1 = sizes
    channels = conv_ref.shape[-1]
    lanes = target_ref.shape[1]
    levels = ((tile0_ref, grad0_ref, side0, 1), (tile1_ref, grad1_ref, side1, base1))

    halves = channels // 128

    def conv_rows(tile_ref, side, base, start, count):
        cells = count * side
        by_tap = []
        for b in range(TAPS):
            parts = []
            for a in range(TAPS):
                block = tile_ref[b, pl.ds(start + a, count)].reshape(cells, channels)
                parts.append(jnp.dot(block, conv_ref[a, b], preferred_element_type=jnp.float32))
            low = parts[0] + parts[1]
            high = parts[1] + parts[2]
            by_tap.append((low + parts[2], high, low))
        for v in range(3):
            low = by_tap[0][v] + by_tap[1][v]
            high = by_tap[1][v] + by_tap[2][v]
            full = low + by_tap[2][v]
            for u, value in enumerate((full, high, low)):
                for half in range(halves):
                    pre_all[v, u, half, pl.ds(start + base, count), 0:side, :] = value[
                        :, half * 128 : (half + 1) * 128
                    ].reshape(count, side, 128)

    for tile_ref, grad_ref, side, base in levels:
        for v in range(3):
            pre_all[v, 0, :, base : base + side, side : side + 8, :] = jnp.zeros(
                (halves, side, 8, 128), jnp.float32
            )
        count = 256 // side

        def step(index, carry, tile_ref=tile_ref, side=side, base=base, count=count):
            conv_rows(tile_ref, side, base, index * count, count)
            return carry

        lax.fori_loop(0, side // count, step, 0)

    for tile_ref, grad_ref, side, base in levels:

        def clear(index, carry, side=side, base=base):
            sums[:, :, :, base - 1 + index, 0:side, :] = jnp.zeros(
                (3, 3, halves, side, 128), jnp.float32
            )
            return carry

        lax.fori_loop(0, side + 2, clear, 0)
    gmask_ref[...] = jnp.zeros_like(gmask_ref)
    logit_all[...] = jnp.zeros_like(logit_all)
    lane = lax.broadcasted_iota(jnp.int32, (ROWS, lanes), 1)
    inside = lax.broadcasted_iota(jnp.int32, (ROWS, lanes), 0) % WIDE < CROP
    first = lax.broadcasted_iota(jnp.int32, (8, 128), 0) == 0
    last = lax.broadcasted_iota(jnp.int32, (8, 128), 0) == CROP - 1 - 8

    def some_crops(group, carry):
        crops = [group * GROUP + k for k in range(GROUP)]
        kinds = [class_ref[entry] for entry in crops]
        rows = [row_ref[entry] for entry in crops]
        cols = [col_ref[entry] for entry in crops]
        class_rows = [mask_ref[pl.ds(jnp.maximum(kind, 0), 1), :] for kind in kinds]
        slopes = []
        hiddens = []
        for k in range(GROUP):
            for i in range(CROP):
                v = line_class(i)
                row = rows[k] + i
                for half in range(halves):
                    near, far = pl.ds(cols[k], 8), pl.ds(cols[k] + 8, 8)
                    width = slice(half * 128, (half + 1) * 128)
                    pre_scr[k, i * WIDE : i * WIDE + 8, width] = jnp.where(
                        first,
                        pre_all[v, 1, half, row, near, :],
                        pre_all[v, 0, half, row, near, :],
                    )
                    pre_scr[k, i * WIDE + 8 : (i + 1) * WIDE, width] = jnp.where(
                        last,
                        pre_all[v, 2, half, row, far, :],
                        pre_all[v, 0, half, row, far, :],
                    )
            pre = pre_scr[k]
            turn = jnp.tanh(pre)
            hidden = pre + pre * turn
            slopes.append(0.25 * ((1.0 + turn) + hidden * (1.0 - turn)))
            hiddens.append((0.5 * hidden).astype(jnp.bfloat16))
        actives = [[] for _ in crops]
        bends = [[] for _ in crops]
        logits = [jnp.zeros((ROWS, lanes), jnp.float32) for _ in crops]
        for q in range(4):
            for k, entry in enumerate(crops):
                up = jnp.dot(hiddens[k], deconv_ref[q], preferred_element_type=jnp.float32)
                turn = jnp.tanh(up)
                active = up + up * turn
                actives[k].append(active)
                bends[k].append(((1.0 + turn) + active * (1.0 - turn)) * class_rows[k])
                value = jnp.sum(active * class_rows[k], axis=1, keepdims=True)
                logits[k] = jnp.where(lane == entry * 4 + q, value, logits[k])
        steep = []
        for k in range(GROUP):
            logit_all[...] += logits[k]
            steep.append(
                jnp.where(
                    inside & (kinds[k] >= 0), sigmoid(logits[k]) - target_ref[...], 0.0
                )
            )
        class_grads = [jnp.zeros((1, channels), jnp.float32) for _ in crops]
        hidden_grads = [jnp.zeros((ROWS, channels), jnp.float32) for _ in crops]
        for q in range(4):
            for k, entry in enumerate(crops):
                one = jnp.sum(
                    jnp.where(lane == entry * 4 + q, steep[k], 0.0), axis=1, keepdims=True
                )
                class_grads[k] += jnp.sum(actives[k][q] * one, axis=0, keepdims=True)
                up_grad = (bends[k][q] * one).astype(jnp.bfloat16)
                hidden_grads[k] += lax.dot_general(
                    up_grad, deconv_ref[q], NT, preferred_element_type=jnp.float32
                )
        for k in range(GROUP):
            gmask_ref[pl.ds(jnp.maximum(kinds[k], 0), 1), :] += class_grads[k]
            pre_grad = (hidden_grads[k] * slopes[k]).astype(jnp.bfloat16).astype(jnp.float32)
            for i in range(CROP):
                v = line_class(i)
                row = rows[k] + i
                for half in range(halves):
                    near, far = pl.ds(cols[k], 8), pl.ds(cols[k] + 8, 8)
                    width = slice(half * 128, (half + 1) * 128)
                    value = pre_grad[i * WIDE : i * WIDE + 8, width]
                    sums[v, 0, half, row, near, :] += jnp.where(first, 0.0, value)
                    sums[v, 1, half, row, near, :] += jnp.where(first, value, 0.0)
                    value = pre_grad[i * WIDE + 8 : (i + 1) * WIDE, width]
                    sums[v, 0, half, row, far, :] += jnp.where(last, 0.0, value)
                    sums[v, 2, half, row, far, :] += jnp.where(last, value, 0.0)
        return carry

    lax.fori_loop(0, entries // GROUP, some_crops, 0)

    logit = logit_all[...]
    loss = jnp.maximum(logit, 0.0) + jnp.log1p(jnp.exp(-jnp.abs(logit)))
    loss = jnp.where(inside, loss - target_ref[...] * logit, 0.0)
    loss = jnp.sum(loss, axis=0, keepdims=True)
    turned[...] = gmask_ref[...].T
    peers = message_ref.shape[0]
    share = channels // peers
    message_ref[...] = jnp.zeros_like(message_ref)
    for peer in range(peers):
        message_ref[peer, 0:share, :] = turned[peer * share : (peer + 1) * share, :]
        for part in range(lanes // 128):
            message_ref[peer, share + part : share + part + 1, :] = loss[
                :, part * 128 : (part + 1) * 128
            ]

    for tile_ref, grad_ref, side, base in levels:
        count = 256 // side
        fold[...] = jnp.zeros_like(fold)

        def step(index, carry, grad_ref=grad_ref, side=side, base=base, count=count):
            cells = count * side
            start = index * count
            totals = [None] * TAPS
            for a in range(TAPS):
                values = [[] for _ in range(TAPS)]
                for half in range(halves):
                    by_tap = [None] * TAPS
                    for v in range(3):
                        if a not in HAS[v]:
                            continue
                        place = pl.ds(start + base + 1 - a, count)
                        full, left, right = (
                            sums[v, u, half, place, 0:side, :] for u in range(3)
                        )
                        low = full + right
                        for b, value in enumerate((low, low + left, full + left)):
                            by_tap[b] = value if by_tap[b] is None else by_tap[b] + value
                    for b in range(TAPS):
                        values[b].append(by_tap[b].reshape(cells, 128).astype(jnp.bfloat16))
                for b in range(TAPS):
                    term = lax.dot_general(
                        jnp.concatenate(values[b], axis=1),
                        conv_ref[a, b],
                        NT,
                        preferred_element_type=jnp.float32,
                    )
                    totals[b] = term if totals[b] is None else totals[b] + term
            for b in range(TAPS):
                fold[b, 0:count, 8 : 8 + side, :] = totals[b].reshape(count, side, channels)
            grad_ref[pl.ds(start, count)] = (
                fold[1, 0:count, 8 : 8 + side, :]
                + fold[0, 0:count, 9 : 9 + side, :]
                + fold[2, 0:count, 7 : 7 + side, :]
            )
            return carry

        lax.fori_loop(0, side // count, step, 0)


def greet(peers, scenes, me, scene):
    barrier = pltpu.get_barrier_semaphore()
    for step in range(1, peers):
        pl.semaphore_signal(
            barrier, inc=1, device_id=(scene, lax.rem(me + step, peers)), device_id_type=MESH
        )
    for step in range(1, scenes):
        pl.semaphore_signal(
            barrier, inc=1, device_id=(lax.rem(scene + step, scenes), me), device_id_type=MESH
        )
    pl.semaphore_wait(barrier, peers + scenes - 2)


def total_kernel(
    sizes, message_ref, out_ref, loss_ref, held, part, others, send1, recv1, send2, recv2
):
    peers, scenes, share = sizes
    me = lax.axis_index("tile")
    scene = lax.axis_index("scene")
    greet(peers, scenes, me, scene)
    copies = []
    for step in range(1, peers):
        peer = lax.rem(me + step, peers)
        copy = pltpu.make_async_remote_copy(
            src_ref=message_ref.at[peer],
            dst_ref=held.at[step],
            send_sem=send1.at[step],
            recv_sem=recv1.at[step],
            device_id=(scene, peer),
            device_id_type=MESH,
        )
        copy.start()
        copies.append(copy)
    own = message_ref[me]
    loss_ref[me] = own[share:]
    total = own[:share]
    for step in range(1, peers):
        copies[step - 1].wait()
        came = held[step]
        loss_ref[lax.rem(me + peers - step, peers)] = came[share:]
        total = total + came[:share]
    part[...] = total
    copies = []
    for step in range(1, scenes):
        copy = pltpu.make_async_remote_copy(
            src_ref=part,
            dst_ref=others.at[step],
            send_sem=send2.at[step],
            recv_sem=recv2.at[step],
            device_id=(lax.rem(scene + step, scenes), me),
            device_id_type=MESH,
        )
        copy.start()
        copies.append(copy)
    for copy in copies:
        copy.wait()
    others[0] = part[...]
    total = others[scene]
    for index in range(1, scenes):
        total = total + others[lax.rem(scene + scenes - index, scenes)]
    out_ref[...] = total


def shifted(tile):
    tile = tile * 0.5
    return jnp.stack(
        [
            jnp.pad(tile, ((1, 1), (1, 0), (0, 0)))[:, :-1],
            jnp.pad(tile, ((1, 1), (0, 0), (0, 0))),
            jnp.pad(tile, ((1, 1), (0, 1), (0, 0)))[:, 1:],
        ]
    )


def on_device(
    level0,
    level1,
    conv_weight,
    deconv_weight,
    mask_weight,
    crop_level,
    crop_row,
    crop_col,
    roi_slot,
    roi_class,
    mask_target,
):
    first_tile = level0[0, 0]
    second_tile = level1[0, 0]
    peers = lax.axis_size("tile")
    entries = crop_level.shape[2]
    per_peer = entries // peers
    channels = first_tile.shape[2]
    side0, side1 = first_tile.shape[0], second_tile.shape[0]
    base1 = side0 + 2
    height = base1 + side1 + 1
    lanes = -(-entries * 4 // 128) * 128
    classes = mask_weight.shape[0]

    slots = roi_slot[0, 0]
    number = slots.shape[0]
    here = slots[None, :] == jnp.arange(entries, dtype=jnp.int32)[:, None]
    targets = (
        mask_target[0, 0]
        .astype(jnp.bfloat16)
        .reshape(number, CROP, 2, CROP, 2)
        .transpose(0, 1, 3, 2, 4)
        .reshape(number, CROP * CROP * 4)
    )
    told = jnp.concatenate(
        [targets, (roi_class[0, 0] + 1).astype(jnp.bfloat16)[:, None]], axis=1
    )
    outgoing = jnp.dot(
        here.astype(jnp.bfloat16), told, preferred_element_type=jnp.float32
    ).astype(jnp.bfloat16)
    outgoing = outgoing.reshape(peers, per_peer, told.shape[1])
    arrived = lax.all_to_all(outgoing, "tile", split_axis=0, concat_axis=0, tiled=True).reshape(
        entries, told.shape[1]
    )
    kinds = arrived[:, -1].astype(jnp.int32) - 1
    target = arrived[:, :-1].reshape(entries, CROP, CROP, 4).transpose(1, 2, 0, 3)
    target = target.reshape(CROP, CROP, entries * 4).astype(jnp.float32)
    target = jnp.pad(target, ((0, 0), (0, WIDE - CROP), (0, lanes - entries * 4)))
    target = target.reshape(ROWS, lanes)

    level = crop_level[0, 0]
    rows = crop_row[0, 0] + jnp.where(level == 0, 1, base1)
    cols = crop_col[0, 0]

    smem = pl.BlockSpec(memory_space=pltpu.SMEM)
    vmem = pl.BlockSpec(memory_space=pltpu.VMEM)
    share = channels // peers
    height_sent = -(-(share + lanes // 128) // 8) * 8
    grad0, grad1, message = pl.pallas_call(
        functools.partial(head_kernel, (side0, side1, entries, base1)),
        out_shape=(
            jax.ShapeDtypeStruct((side0, side0, channels), jnp.float32),
            jax.ShapeDtypeStruct((side1, side1, channels), jnp.float32),
            jax.ShapeDtypeStruct((peers, height_sent, 128), jnp.float32),
        ),
        in_specs=[smem] * 3 + [vmem] * 6,
        out_specs=(vmem,) * 3,
        scratch_shapes=[
            pltpu.VMEM((3, 3, channels // 128, height, side0 + 8, 128), jnp.float32),
            pltpu.VMEM((3, 3, channels // 128, height, side0 + 8, 128), jnp.float32),
            pltpu.VMEM((3, 256 // side1, side0 + 16, channels), jnp.float32),
            pltpu.VMEM((ROWS, lanes), jnp.float32),
            pltpu.VMEM((GROUP, ROWS, channels), jnp.float32),
            pltpu.VMEM((128, channels), jnp.float32),
            pltpu.VMEM((channels, 128), jnp.float32),
        ],
        compiler_params=pltpu.CompilerParams(vmem_limit_bytes=60 * 1024 * 1024),
    )(
        rows,
        cols,
        kinds,
        shifted(first_tile),
        shifted(second_tile),
        conv_weight,
        deconv_weight.reshape(4, channels, channels),
        mask_weight.astype(jnp.float32),
        target,
    )

    scenes = lax.axis_size("scene")
    gmask, loss_rows = pl.pallas_call(
        functools.partial(total_kernel, (peers, scenes, share)),
        out_shape=(
            jax.ShapeDtypeStruct((share, 128), jnp.float32),
            jax.ShapeDtypeStruct((peers, height_sent - share, 128), jnp.float32),
        ),
        in_specs=[vmem],
        out_specs=(vmem,) * 2,
        scratch_shapes=[
            pltpu.VMEM((peers, height_sent, 128), jnp.float32),
            pltpu.VMEM((share, 128), jnp.float32),
            pltpu.VMEM((scenes, share, 128), jnp.float32),
            pltpu.SemaphoreType.DMA((peers,)),
            pltpu.SemaphoreType.DMA((peers,)),
            pltpu.SemaphoreType.DMA((scenes,)),
            pltpu.SemaphoreType.DMA((scenes,)),
        ],
        compiler_params=pltpu.CompilerParams(collective_id=1, has_side_effects=True),
    )(message)
    mask_part = gmask[:, :classes].T
    loss_rows = loss_rows[:, : lanes // 128].reshape(peers, lanes)
    losses = lax.dynamic_slice_in_dim(
        loss_rows, lax.axis_index("tile") * (per_peer * 4), per_peer * 4, axis=1
    )
    losses = losses.reshape(entries, 4).sum(axis=1) / (4 * CROP * CROP)
    losses = jnp.sum(jnp.where(here, losses[:, None], 0.0), axis=0)
    return (grad0[None, None], grad1[None, None], mask_part, losses[None, None])


def solution(mesh):
    in_specs = (
        P("scene", "tile", None, None, None),
        P("scene", "tile", None, None, None),
        P(),
        P(),
        P(),
        P("scene", "tile", None),
        P("scene", "tile", None),
        P("scene", "tile", None),
        P("scene", "tile", None),
        P("scene", "tile", None),
        P("scene", "tile", None, None, None),
    )
    out_specs = (
        P("scene", "tile", None, None, None),
        P("scene", "tile", None, None, None),
        P(None, "tile"),
        P("scene", "tile", None),
    )
    return jax.shard_map(
        on_device, mesh=mesh, in_specs=in_specs, out_specs=out_specs, check_vma=False
    )
```

```python
import functools

import jax
import jax.numpy as jnp
from jax import lax
from jax.experimental import pallas as pl
from jax.experimental.pallas import tpu as pltpu
from jax.sharding import PartitionSpec as P

CROP = 14
WIDE = 16
GROUP = 4
ROWS = CROP * WIDE
TAPS = 3
MESH = pl.DeviceIdType.MESH
NT = (((1,), (1,)), ((), ()))
HAS = ((0, 1, 2), (1, 2), (0, 1))


def sigmoid(values):
    return 0.5 + 0.5 * jnp.tanh(0.5 * values)


def line_class(index):
    return 1 if index == 0 else (2 if index == CROP - 1 else 0)


def head_kernel(
    sizes,
    row_ref,
    col_ref,
    class_ref,
    level_ref,
    raw0_ref,
    raw1_ref,
    conv_ref,
    deconv_ref,
    weight_ref,
    target_ref,
    grad0_ref,
    grad1_ref,
    message_ref,
    pre_all,
    sums,
    fold,
    logit_all,
    pre_scr,
    gmask_ref,
    turned,
    mask_ref,
    tile0_ref,
    tile1_ref,
):
    side0, side1, entries, base1 = sizes
    channels = conv_ref.shape[-1]
    lanes = target_ref.shape[1]
    levels = ((tile0_ref, grad0_ref, side0, 1), (tile1_ref, grad1_ref, side1, base1))

    halves = channels // 128
    mask_ref[...] = weight_ref[...].astype(jnp.float32)

    for raw_ref, tile_ref, side in ((raw0_ref, tile0_ref, side0), (raw1_ref, tile1_ref, side1)):
        for edge in (0, side + 1):
            tile_ref[:, edge] = jnp.zeros((TAPS, side, channels), jnp.bfloat16)
        count = 256 // side
        place = lax.broadcasted_iota(jnp.int32, (256, channels), 0) % side

        def spread(index, carry, raw_ref=raw_ref, tile_ref=tile_ref, side=side, count=count, place=place):
            start = index * count
            value = raw_ref[pl.ds(start, count)].astype(jnp.float32) * 0.5
            value = value.reshape(256, channels)
            moved = (
                jnp.where(place == 0, 0.0, pltpu.roll(value, 1, 0)),
                value,
                jnp.where(place == side - 1, 0.0, pltpu.roll(value, 255, 0)),
            )
            for b in range(TAPS):
                tile_ref[b, pl.ds(start + 1, count)] = (
                    moved[b].astype(jnp.bfloat16).reshape(count, side, channels)
                )
            return carry

        lax.fori_loop(0, side // count, spread, 0)

    def conv_rows(tile_ref, side, base, start, count):
        cells = count * side
        by_tap = []
        for b in range(TAPS):
            parts = []
            for a in range(TAPS):
                block = tile_ref[b, pl.ds(start + a, count)].reshape(cells, channels)
                parts.append(jnp.dot(block, conv_ref[a, b], preferred_element_type=jnp.float32))
            low = parts[0] + parts[1]
            high = parts[1] + parts[2]
            by_tap.append((low + parts[2], high, low))
        for v in range(3):
            low = by_tap[0][v] + by_tap[1][v]
            high = by_tap[1][v] + by_tap[2][v]
            full = low + by_tap[2][v]
            for u, value in enumerate((full, high, low)):
                for half in range(halves):
                    pre_all[v, u, half, pl.ds(start + base, count), 0:side, :] = value[
                        :, half * 128 : (half + 1) * 128
                    ].reshape(count, side, 128)

    for tile_ref, grad_ref, side, base in levels:
        for v in range(3):
            pre_all[v, 0, :, base : base + side, side : side + 8, :] = jnp.zeros(
                (halves, side, 8, 128), jnp.float32
            )
        count = 256 // side

        def step(index, carry, tile_ref=tile_ref, side=side, base=base, count=count):
            conv_rows(tile_ref, side, base, index * count, count)
            return carry

        lax.fori_loop(0, side // count, step, 0)

    for tile_ref, grad_ref, side, base in levels:

        def clear(index, carry, side=side, base=base):
            sums[:, :, :, base - 1 + index, 0:side, :] = jnp.zeros(
                (3, 3, halves, side, 128), jnp.float32
            )
            return carry

        lax.fori_loop(0, side + 2, clear, 0)
    gmask_ref[...] = jnp.zeros_like(gmask_ref)
    logit_all[...] = jnp.zeros_like(logit_all)
    lane = lax.broadcasted_iota(jnp.int32, (ROWS, lanes), 1)
    inside = lax.broadcasted_iota(jnp.int32, (ROWS, lanes), 0) % WIDE < CROP
    first = lax.broadcasted_iota(jnp.int32, (8, 128), 0) == 0
    last = lax.broadcasted_iota(jnp.int32, (8, 128), 0) == CROP - 1 - 8

    def some_crops(group, carry):
        crops = [group * GROUP + k for k in range(GROUP)]
        kinds = [class_ref[entry] for entry in crops]
        rows = [row_ref[entry] + jnp.where(level_ref[entry] == 0, 1, base1) for entry in crops]
        cols = [col_ref[entry] for entry in crops]
        class_rows = [mask_ref[pl.ds(jnp.maximum(kind, 0), 1), :] for kind in kinds]
        slopes = []
        hiddens = []
        for k in range(GROUP):
            for i in range(CROP):
                v = line_class(i)
                row = rows[k] + i
                for half in range(halves):
                    near, far = pl.ds(cols[k], 8), pl.ds(cols[k] + 8, 8)
                    width = slice(half * 128, (half + 1) * 128)
                    pre_scr[k, i * WIDE : i * WIDE + 8, width] = jnp.where(
                        first,
                        pre_all[v, 1, half, row, near, :],
                        pre_all[v, 0, half, row, near, :],
                    )
                    pre_scr[k, i * WIDE + 8 : (i + 1) * WIDE, width] = jnp.where(
                        last,
                        pre_all[v, 2, half, row, far, :],
                        pre_all[v, 0, half, row, far, :],
                    )
            pre = pre_scr[k]
            turn = jnp.tanh(pre)
            hidden = pre + pre * turn
            slopes.append(0.25 * ((1.0 + turn) + hidden * (1.0 - turn)))
            hiddens.append((0.5 * hidden).astype(jnp.bfloat16))
        actives = [[] for _ in crops]
        bends = [[] for _ in crops]
        logits = [jnp.zeros((ROWS, lanes), jnp.float32) for _ in crops]
        for q in range(4):
            for k, entry in enumerate(crops):
                up = jnp.dot(hiddens[k], deconv_ref[q], preferred_element_type=jnp.float32)
                turn = jnp.tanh(up)
                active = up + up * turn
                actives[k].append(active)
                bends[k].append(((1.0 + turn) + active * (1.0 - turn)) * class_rows[k])
                value = jnp.sum(active * class_rows[k], axis=1, keepdims=True)
                logits[k] = jnp.where(lane == entry * 4 + q, value, logits[k])
        steep = []
        for k in range(GROUP):
            logit_all[...] += logits[k]
            steep.append(
                jnp.where(
                    inside & (kinds[k] >= 0), sigmoid(logits[k]) - target_ref[...], 0.0
                )
            )
        class_grads = [jnp.zeros((1, channels), jnp.float32) for _ in crops]
        hidden_grads = [jnp.zeros((ROWS, channels), jnp.float32) for _ in crops]
        for q in range(4):
            for k, entry in enumerate(crops):
                one = jnp.sum(
                    jnp.where(lane == entry * 4 + q, steep[k], 0.0), axis=1, keepdims=True
                )
                class_grads[k] += jnp.sum(actives[k][q] * one, axis=0, keepdims=True)
                up_grad = (bends[k][q] * one).astype(jnp.bfloat16)
                hidden_grads[k] += lax.dot_general(
                    up_grad, deconv_ref[q], NT, preferred_element_type=jnp.float32
                )
        for k in range(GROUP):
            gmask_ref[pl.ds(jnp.maximum(kinds[k], 0), 1), :] += class_grads[k]
            pre_grad = (hidden_grads[k] * slopes[k]).astype(jnp.bfloat16).astype(jnp.float32)
            for i in range(CROP):
                v = line_class(i)
                row = rows[k] + i
                for half in range(halves):
                    near, far = pl.ds(cols[k], 8), pl.ds(cols[k] + 8, 8)
                    width = slice(half * 128, (half + 1) * 128)
                    value = pre_grad[i * WIDE : i * WIDE + 8, width]
                    sums[v, 0, half, row, near, :] += jnp.where(first, 0.0, value)
                    sums[v, 1, half, row, near, :] += jnp.where(first, value, 0.0)
                    value = pre_grad[i * WIDE + 8 : (i + 1) * WIDE, width]
                    sums[v, 0, half, row, far, :] += jnp.where(last, 0.0, value)
                    sums[v, 2, half, row, far, :] += jnp.where(last, value, 0.0)
        return carry

    lax.fori_loop(0, entries // GROUP, some_crops, 0)

    logit = logit_all[...]
    loss = jnp.maximum(logit, 0.0) + jnp.log1p(jnp.exp(-jnp.abs(logit)))
    loss = jnp.where(inside, loss - target_ref[...] * logit, 0.0)
    loss = jnp.sum(loss, axis=0, keepdims=True)
    turned[...] = gmask_ref[...].T
    peers = message_ref.shape[0]
    share = channels // peers
    message_ref[...] = jnp.zeros_like(message_ref)
    for peer in range(peers):
        message_ref[peer, 0:share, :] = turned[peer * share : (peer + 1) * share, :]
        for part in range(lanes // 128):
            message_ref[peer, share + part : share + part + 1, :] = loss[
                :, part * 128 : (part + 1) * 128
            ]

    for tile_ref, grad_ref, side, base in levels:
        count = 256 // side
        fold[...] = jnp.zeros_like(fold)

        def step(index, carry, grad_ref=grad_ref, side=side, base=base, count=count):
            cells = count * side
            start = index * count
            totals = [None] * TAPS
            for a in range(TAPS):
                values = [[] for _ in range(TAPS)]
                for half in range(halves):
                    by_tap = [None] * TAPS
                    for v in range(3):
                        if a not in HAS[v]:
                            continue
                        place = pl.ds(start + base + 1 - a, count)
                        full, left, right = (
                            sums[v, u, half, place, 0:side, :] for u in range(3)
                        )
                        low = full + right
                        for b, value in enumerate((low, low + left, full + left)):
                            by_tap[b] = value if by_tap[b] is None else by_tap[b] + value
                    for b in range(TAPS):
                        values[b].append(by_tap[b].reshape(cells, 128).astype(jnp.bfloat16))
                for b in range(TAPS):
                    term = lax.dot_general(
                        jnp.concatenate(values[b], axis=1),
                        conv_ref[a, b],
                        NT,
                        preferred_element_type=jnp.float32,
                    )
                    totals[b] = term if totals[b] is None else totals[b] + term
            for b in range(TAPS):
                fold[b, 0:count, 8 : 8 + side, :] = totals[b].reshape(count, side, channels)
            grad_ref[pl.ds(start, count)] = (
                fold[1, 0:count, 8 : 8 + side, :]
                + fold[0, 0:count, 9 : 9 + side, :]
                + fold[2, 0:count, 7 : 7 + side, :]
            )
            return carry

        lax.fori_loop(0, side // count, step, 0)


def greet(peers, scenes, me, scene):
    barrier = pltpu.get_barrier_semaphore()
    for step in range(1, peers):
        pl.semaphore_signal(
            barrier, inc=1, device_id=(scene, lax.rem(me + step, peers)), device_id_type=MESH
        )
    for step in range(1, scenes):
        pl.semaphore_signal(
            barrier, inc=1, device_id=(lax.rem(scene + step, scenes), me), device_id_type=MESH
        )
    pl.semaphore_wait(barrier, peers + scenes - 2)


def total_kernel(
    sizes, message_ref, out_ref, loss_ref, held, part, others, send1, recv1, send2, recv2
):
    peers, scenes, share = sizes
    me = lax.axis_index("tile")
    scene = lax.axis_index("scene")
    greet(peers, scenes, me, scene)
    copies = []
    for step in range(1, peers):
        peer = lax.rem(me + step, peers)
        copy = pltpu.make_async_remote_copy(
            src_ref=message_ref.at[peer],
            dst_ref=held.at[step],
            send_sem=send1.at[step],
            recv_sem=recv1.at[step],
            device_id=(scene, peer),
            device_id_type=MESH,
        )
        copy.start()
        copies.append(copy)
    own = message_ref[me]
    loss_ref[me] = own[share:]
    total = own[:share]
    for step in range(1, peers):
        copies[step - 1].wait()
        came = held[step]
        loss_ref[lax.rem(me + peers - step, peers)] = came[share:]
        total = total + came[:share]
    part[...] = total
    copies = []
    for step in range(1, scenes):
        copy = pltpu.make_async_remote_copy(
            src_ref=part,
            dst_ref=others.at[step],
            send_sem=send2.at[step],
            recv_sem=recv2.at[step],
            device_id=(lax.rem(scene + step, scenes), me),
            device_id_type=MESH,
        )
        copy.start()
        copies.append(copy)
    for copy in copies:
        copy.wait()
    others[0] = part[...]
    total = others[scene]
    for index in range(1, scenes):
        total = total + others[lax.rem(scene + scenes - index, scenes)]
    out_ref[...] = total


def on_device(
    level0,
    level1,
    conv_weight,
    deconv_weight,
    mask_weight,
    crop_level,
    crop_row,
    crop_col,
    roi_slot,
    roi_class,
    mask_target,
):
    first_tile = level0[0, 0]
    second_tile = level1[0, 0]
    peers = lax.axis_size("tile")
    entries = crop_level.shape[2]
    per_peer = entries // peers
    channels = first_tile.shape[2]
    side0, side1 = first_tile.shape[0], second_tile.shape[0]
    base1 = side0 + 2
    height = base1 + side1 + 1
    lanes = -(-entries * 4 // 128) * 128
    classes = mask_weight.shape[0]

    slots = roi_slot[0, 0]
    number = slots.shape[0]
    here = slots[None, :] == jnp.arange(entries, dtype=jnp.int32)[:, None]
    targets = (
        mask_target[0, 0]
        .astype(jnp.bfloat16)
        .reshape(number, CROP, 2, CROP, 2)
        .transpose(0, 1, 3, 2, 4)
        .reshape(number, CROP * CROP * 4)
    )
    told = jnp.concatenate(
        [targets, (roi_class[0, 0] + 1).astype(jnp.bfloat16)[:, None]], axis=1
    )
    outgoing = jnp.dot(
        here.astype(jnp.bfloat16), told, preferred_element_type=jnp.float32
    ).astype(jnp.bfloat16)
    outgoing = outgoing.reshape(peers, per_peer, told.shape[1])
    arrived = lax.all_to_all(outgoing, "tile", split_axis=0, concat_axis=0, tiled=True).reshape(
        entries, told.shape[1]
    )
    kinds = arrived[:, -1].astype(jnp.int32) - 1
    target = arrived[:, :-1].reshape(entries, CROP, CROP, 4).transpose(1, 2, 0, 3)
    target = target.reshape(CROP, CROP, entries * 4).astype(jnp.float32)
    target = jnp.pad(target, ((0, 0), (0, WIDE - CROP), (0, lanes - entries * 4)))
    target = target.reshape(ROWS, lanes)

    smem = pl.BlockSpec(memory_space=pltpu.SMEM)
    vmem = pl.BlockSpec(memory_space=pltpu.VMEM)
    share = channels // peers
    height_sent = -(-(share + lanes // 128) // 8) * 8
    grad0, grad1, message = pl.pallas_call(
        functools.partial(head_kernel, (side0, side1, entries, base1)),
        out_shape=(
            jax.ShapeDtypeStruct((side0, side0, channels), jnp.float32),
            jax.ShapeDtypeStruct((side1, side1, channels), jnp.float32),
            jax.ShapeDtypeStruct((peers, height_sent, 128), jnp.float32),
        ),
        in_specs=[smem] * 4 + [vmem] * 6,
        out_specs=(vmem,) * 3,
        scratch_shapes=[
            pltpu.VMEM((3, 3, channels // 128, height, side0 + 8, 128), jnp.float32),
            pltpu.VMEM((3, 3, channels // 128, height, side0 + 8, 128), jnp.float32),
            pltpu.VMEM((3, 256 // side1, side0 + 16, channels), jnp.float32),
            pltpu.VMEM((ROWS, lanes), jnp.float32),
            pltpu.VMEM((GROUP, ROWS, channels), jnp.float32),
            pltpu.VMEM((128, channels), jnp.float32),
            pltpu.VMEM((channels, 128), jnp.float32),
            pltpu.VMEM((classes, channels), jnp.float32),
            pltpu.VMEM((TAPS, side0 + 2, side0, channels), jnp.bfloat16),
            pltpu.VMEM((TAPS, side1 + 2, side1, channels), jnp.bfloat16),
        ],
        compiler_params=pltpu.CompilerParams(vmem_limit_bytes=60 * 1024 * 1024),
    )(
        crop_row[0, 0],
        crop_col[0, 0],
        kinds,
        crop_level[0, 0],
        first_tile,
        second_tile,
        conv_weight,
        deconv_weight.reshape(4, channels, channels),
        mask_weight,
        target,
    )

    scenes = lax.axis_size("scene")
    gmask, loss_rows = pl.pallas_call(
        functools.partial(total_kernel, (peers, scenes, share)),
        out_shape=(
            jax.ShapeDtypeStruct((share, 128), jnp.float32),
            jax.ShapeDtypeStruct((peers, height_sent - share, 128), jnp.float32),
        ),
        in_specs=[vmem],
        out_specs=(vmem,) * 2,
        scratch_shapes=[
            pltpu.VMEM((peers, height_sent, 128), jnp.float32),
            pltpu.VMEM((share, 128), jnp.float32),
            pltpu.VMEM((scenes, share, 128), jnp.float32),
            pltpu.SemaphoreType.DMA((peers,)),
            pltpu.SemaphoreType.DMA((peers,)),
            pltpu.SemaphoreType.DMA((scenes,)),
            pltpu.SemaphoreType.DMA((scenes,)),
        ],
        compiler_params=pltpu.CompilerParams(collective_id=1, has_side_effects=True),
    )(message)
    mask_part = gmask[:, :classes].T
    loss_rows = loss_rows[:, : lanes // 128].reshape(peers, lanes)
    losses = lax.dynamic_slice_in_dim(
        loss_rows, lax.axis_index("tile") * (per_peer * 4), per_peer * 4, axis=1
    )
    losses = losses.reshape(entries, 4).sum(axis=1) / (4 * CROP * CROP)
    losses = jnp.sum(jnp.where(here, losses[:, None], 0.0), axis=0)
    return (grad0[None, None], grad1[None, None], mask_part, losses[None, None])


def solution(mesh):
    in_specs = (
        P("scene", "tile", None, None, None),
        P("scene", "tile", None, None, None),
        P(),
        P(),
        P(),
        P("scene", "tile", None),
        P("scene", "tile", None),
        P("scene", "tile", None),
        P("scene", "tile", None),
        P("scene", "tile", None),
        P("scene", "tile", None, None, None),
    )
    out_specs = (
        P("scene", "tile", None, None, None),
        P("scene", "tile", None, None, None),
        P(None, "tile"),
        P("scene", "tile", None),
    )
    return jax.shard_map(
        on_device, mesh=mesh, in_specs=in_specs, out_specs=out_specs, check_vma=False
    )
```
